32 devices in a mesh: groups: 2 (over x), chan: 16 (over z, y, core).
Axes of the slice: x: 2, y: 2, z: 4, core: 2. Of those that a mesh axis runs over, the one named last changes fastest.
Arguments:
- raw: bfloat16 [5120, 4096], P('chan', 'groups'), parts along dimension 1, may hold values from -50 to 50
- taps: bfloat16 [255], replicated, may hold values from -0.375 to 0.375
- tile_dist: int32 [16, 8], P('chan', 'groups'), parts along dimension 1, may hold values from 1 to 4, as said below
- tile_count: int32 [32], P(('groups', 'chan')), parts along dimension 0, may hold values from 0 to 4
- owner: int32 [8], P('groups'), parts along dimension 0, may hold values from 0 to 15, as said below
Outputs:
- band_stack: float32 [16, 256, 128], P('chan', 'groups'), parts along dimension 1
The draws below stay inside these ranges and needn't reach their ends.
There are 2 independent parts, one for each index of `groups`. The reference program is written for one: setup_inputs(seed, part) draws one part's arguments, and reference() takes and returns one part's arrays. A program takes and returns all parts, laid end to end along the dimension named above; an argument that names none is the same for every part. Nothing has to cross between parts.
Inputs may be any that keep to these rules, and one draw needn't show every extreme that they name: Each row of tile_dist holds every distance of 1 to 4 once; in row i the first tile_count[i] entries d satisfy i + d < 16. `owner`: the owners are distinct, and some band is owned by index 15.
All inputs are finite; a program needn't handle non-finite values.
Results may differ from the reference program's by a relative error of at most 0.014.
Values may be sent and summed in bfloat16 or wider, within the bound.
A program may use at most 128 MiB of HBM per device.

```python
import math
import jax
import jax.numpy as jnp
from jax import lax

CB = 128
NB = 4
TAPS = 255
CH = 2048
TIME = 5120
BINS = 64
HALF = 127
N_CHAN = 16


def draw_raw(key, part):
    first, second = jax.random.split(key, 2)
    level = jnp.exp(jax.random.uniform(first, (1, CH), jnp.float32, 0.0, math.log(10.0)))
    noise = jnp.clip(jax.random.normal(second, (TIME, CH), jnp.float32), -5.0, 5.0)
    return (noise * level).astype(jnp.bfloat16)


def tile_plan(key):
    base = jax.random.fold_in(key, 7)
    ranks = jax.random.randint(jax.random.fold_in(base, 1), (N_CHAN, NB), 0, 1 << 20)
    lanes = jnp.arange(NB, dtype=jnp.int32)
    device = jnp.arange(N_CHAN, dtype=jnp.int32)[:, None]
    invalid = (device + lanes[None, :] + 1 >= N_CHAN).astype(jnp.int32)
    score = invalid * (1 << 28) + ranks * NB + lanes[None, :]
    order = jnp.argsort(score, axis=1).astype(jnp.int32)
    distances = order + 1
    usable = NB - jnp.sum(invalid, axis=1)
    draws = jax.random.randint(jax.random.fold_in(base, 2), (N_CHAN,), 0, NB)
    counts = 1 + draws * draws * (NB - 1) // ((NB - 1) * (NB - 1))
    counts = jnp.where(device[:, 0] == 0, NB, counts)
    counts = jnp.minimum(counts, usable).astype(jnp.int32)
    return (distances, counts)


def draw_tile_dist(key, part):
    return tile_plan(key)[0]


def draw_tile_count(key, part):
    return tile_plan(key)[1]


def draw_owner(key, part):
    others = jax.random.permutation(jax.random.fold_in(key, 19), N_CHAN - 1)[:NB - 1].astype(jnp.int32)
    values = jnp.concatenate([others, jnp.full((1,), N_CHAN - 1, jnp.int32)])
    order = jax.random.permutation(jax.random.fold_in(key, 23), NB).astype(jnp.int32)
    return values[order].astype(jnp.int32)


def bell_draw(own_key, dims, spread, bound, kind=jnp.bfloat16):
    values = jax.random.normal(own_key, dims, jnp.float32) * spread
    return jnp.minimum(jnp.maximum(values, -bound), bound).astype(kind)


def setup_inputs(seed: int = 0, part: int = 0) -> dict:
    streams_of = jax.random.split(jax.random.key(seed), 6)
    own_keys = jax.random.split(jax.random.fold_in(streams_of[5], part), 6)
    raw = draw_raw(jax.random.fold_in(jax.random.fold_in(streams_of[5], part), 71), part)
    taps = bell_draw(streams_of[1], (TAPS,), TAPS ** -0.5, 0.375)
    tile_dist = draw_tile_dist(jax.random.fold_in(jax.random.fold_in(streams_of[5], part), 71), part)
    tile_count = draw_tile_count(jax.random.fold_in(jax.random.fold_in(streams_of[5], part), 71), part)
    owner = draw_owner(jax.random.fold_in(jax.random.fold_in(streams_of[5], part), 71), part)
    return dict(raw=raw, taps=taps, tile_dist=tile_dist, tile_count=tile_count, owner=owner)


def reference(raw, taps, tile_dist, tile_count, owner):
    length = 1 << (TIME + TAPS - 2).bit_length()
    flipped = taps.astype(jnp.float32)[::-1]
    response = jnp.fft.rfft(flipped, length)

    def block_spectra(index):
        start = (index * CB).astype(jnp.int32)
        block = lax.dynamic_slice_in_dim(raw, start, CB, 1).astype(jnp.float32)
        full = jnp.fft.irfft(jnp.fft.rfft(block, length, axis=0) * response[:, None], length, axis=0)
        decimated = full[HALF:HALF + TIME:5].astype(jnp.float32).astype(jnp.bfloat16)
        spectrum = jnp.fft.rfft(decimated.astype(jnp.float32), axis=0)[1:BINS + 1]
        real_part = jnp.real(spectrum).astype(jnp.float32)
        imag_part = jnp.imag(spectrum).astype(jnp.float32)
        stacked = jnp.concatenate([real_part, imag_part], axis=0)
        power = lax.optimization_barrier(jnp.sum(real_part * real_part + imag_part * imag_part, axis=1)) / (2 * CB)
        gain = lax.rsqrt(power + 1e-06)
        return (stacked * jnp.concatenate([gain, gain])[:, None]).astype(jnp.bfloat16)
    spectra = lax.map(block_spectra, jnp.arange(N_CHAN, dtype=jnp.int32))
    slots = jnp.arange(NB, dtype=jnp.int32)[None, :] < tile_count[:, None]
    scale = 1.0 / (2 * BINS)
    stacks = []
    for distance in range(1, NB + 1):
        listed = lax.optimization_barrier(jnp.sum((slots & (tile_dist == distance)).astype(jnp.float32), axis=1))
        left = spectra[:N_CHAN - distance].astype(jnp.float32) * listed[:N_CHAN - distance, None, None]
        right = spectra[distance:].astype(jnp.float32)
        stacks.append(jnp.einsum('iea,ieb->ab', left, right, precision=lax.Precision.HIGHEST) * scale)
    stacked = jnp.stack(stacks)
    places = (owner[:, None] == jnp.arange(N_CHAN, dtype=jnp.int32)[None, :]).astype(jnp.float32)
    return jnp.einsum('bn,bxy->nxy', places, stacked, precision=lax.Precision.HIGHEST)
```

```python
import functools
import math

import jax
import jax.numpy as jnp
from jax import lax
from jax.experimental import pallas as pl
from jax.experimental.pallas import tpu as pltpu
from jax.sharding import PartitionSpec as P

MESH = pl.DeviceIdType.MESH


def extended(x, sides, width):
    for axis, dim in sides:
        size, length = (lax.axis_size(axis), x.shape[dim])
        up = [(i, (i + 1) % size) for i in range(size - 1)]
        down = [(j, i) for i, j in up]
        last = lax.slice_in_dim(x, length - width, length, axis=dim)
        initial = lax.slice_in_dim(x, 0, width, axis=dim)
        before = lax.ppermute(last, axis, up)
        after = lax.ppermute(initial, axis, down)
        x = jnp.concatenate([before, x, after], axis=dim)
    return x


def passed_along(x, axis, by):
    size = lax.axis_size(axis)
    pairs = [(i, i + by) for i in range(size) if 0 <= i + by < size]
    return lax.ppermute(x, axis, pairs)


def band_matrix(taps, out_rows, in_cols):
    period = in_cols + 5
    padded = jnp.pad(taps, (0, period - taps.shape[0]))
    return jnp.tile(padded, out_rows)[: out_rows * in_cols].reshape(out_rows, in_cols)


def whiten(block):
    length, channels = block.shape
    bins = length // 16
    freqs = jnp.arange(1, bins + 1, dtype=jnp.int32)[:, None]
    times = jnp.arange(length, dtype=jnp.int32)[None, :]
    angle = (freqs * times % length).astype(jnp.float32) * (2.0 * math.pi / length)
    table = jnp.concatenate([jnp.cos(angle), -jnp.sin(angle)], axis=0)
    table_high = table.astype(jnp.bfloat16)
    table_low = (table - table_high.astype(jnp.float32)).astype(jnp.bfloat16)
    spectrum = jnp.dot(table_high, block, preferred_element_type=jnp.float32)
    spectrum = spectrum + jnp.dot(table_low, block, preferred_element_type=jnp.float32)
    squares = spectrum * spectrum
    power = jnp.sum(squares[:bins] + squares[bins:], axis=1) / (2 * channels)
    gain = lax.rsqrt(power + 1e-06)
    return (spectrum * jnp.concatenate([gain, gain])[:, None]).astype(jnp.bfloat16)


def cross_tile(mine, partner, scale):
    product = lax.dot_general(
        mine, partner, (((0,), (0,)), ((), ())), preferred_element_type=jnp.float32
    )
    return product * scale


def streamed(raw, taps, tile_dist, tile_count, owner):
    rows = raw.shape[0]
    width = taps.shape[0]
    half = (width - 1) // 2
    out_rows = rows // 5
    banded = band_matrix(taps, out_rows, rows + 2 * half)
    padded = extended(raw, (("chan", 0),), half)
    filtered = jnp.dot(banded, padded, preferred_element_type=jnp.float32)
    decimated = filtered.astype(jnp.bfloat16)
    regrouped = lax.all_to_all(decimated, "chan", split_axis=1, concat_axis=0, tiled=True)
    whitened = whiten(regrouped)
    channels = whitened.shape[1]
    scale = 1.0 / whitened.shape[0]
    bands = tile_dist.shape[1]
    slots = jnp.arange(bands, dtype=jnp.int32) < tile_count[0]
    stacks = []
    for distance in range(1, bands + 1):
        partner = passed_along(whitened, "chan", -distance)
        listed = jnp.sum(((tile_dist[0] == distance) & slots).astype(jnp.int32))
        tile = lax.cond(
            listed > 0,
            lambda first, second: cross_tile(first, second, scale),
            lambda first, second: jnp.zeros((channels, channels), jnp.float32),
            whitened,
            partner,
        )
        stacks.append(tile)
    stacked = jnp.stack(stacks)
    totals = lax.psum(stacked, "chan")
    selected = (owner == lax.axis_index("chan")).astype(jnp.float32)
    return jnp.einsum("b,bxy->xy", selected, totals, precision=lax.Precision.HIGHEST)[None]


def split(x):
    high = x.astype(jnp.bfloat16)
    low = (x - high.astype(jnp.float32)).astype(jnp.bfloat16)
    return high, low


def mm(a, b):
    return jnp.dot(a, b, preferred_element_type=jnp.float32)


def fused_kernel(
    n, width, bands,
    dist_ref, count_ref, owner_ref, raw_ref, taps_ref, out_ref,
    send1, recv1, send2, recv2, send3, ss1, rs1, ss2, rs2, ss3, rs3,
):
    me = lax.axis_index("chan")
    rows, channels = raw_ref.shape
    block = channels // n
    steps = rows // 5
    length = steps * n
    bins = length // 16
    mine = 2 * bins // n
    hc = channels // 2
    window = 128
    lead = (window - steps) // 2

    barrier = pltpu.get_barrier_semaphore()
    for k in range(1, n):
        pl.semaphore_signal(
            barrier, inc=1, device_id={"chan": lax.rem(me + k, n)}, device_id_type=MESH
        )

    lanes = taps_ref.shape[1]
    first = pltpu.roll(taps_ref[...], 0, 1, stride=5, stride_axis=0)
    banded = jnp.concatenate(
        [pltpu.roll(first, 40 * q, 1)[:, :384] for q in range(window // 8)], axis=0
    ).astype(jnp.bfloat16)[:, :rows]
    row = lax.broadcasted_iota(jnp.int32, (2 * bins, window), 0)
    col = lax.broadcasted_iota(jnp.int32, (2 * bins, window), 1)
    place = row % mine
    freq = (row // mine) * (mine // 2) + place % (mine // 2) + 1
    time = me * steps - lead + col
    turn = (freq * time + jnp.where(place >= mine // 2, length // 4, 0)) & (length - 1)
    table = jnp.cos(turn.astype(jnp.float32) * (2.0 * math.pi / length))
    table = jnp.where((time >= 0) & (time < length), table, 0.0)
    table_high, table_low = split(table)
    gmap = mm(table_high, banded) + mm(table_low, banded)
    gmap_high, gmap_low = split(gmap)

    chunk = 256
    for c in range(hc // chunk):
        halves = []
        for h in range(2):
            part = raw_ref[:, h * hc + c * chunk : h * hc + (c + 1) * chunk]
            spectra = mm(gmap_high, part) + mm(gmap_low, part)
            halves.append(spectra.reshape(n, mine, chunk))
        send1[:, :, c * chunk : (c + 1) * chunk] = jnp.concatenate(halves, axis=1).astype(
            jnp.bfloat16
        )
    line = lax.broadcasted_iota(jnp.int32, (2 * mine, 128), 0)
    info = jnp.zeros((2 * mine, 128), jnp.float32)
    for d in range(bands):
        listed = jnp.int32(0)
        for s in range(bands):
            hit = (dist_ref[0, s] == d + 1) & (s < count_ref[0])
            listed = listed + hit.astype(jnp.int32)
        info = jnp.where(line == d, listed.astype(jnp.float32), info)
    send1[:, :, hc:] = jnp.broadcast_to(info[None], (n, 2 * mine, 128)).astype(jnp.bfloat16)

    pl.semaphore_wait(barrier, n - 1)

    def copy1(k):
        to = lax.rem(me + k, n)
        return pltpu.make_async_remote_copy(
            src_ref=send1.at[to], dst_ref=recv1.at[me], send_sem=ss1.at[k],
            recv_sem=rs1.at[k], device_id={"chan": to}, device_id_type=MESH,
        )

    def copy2(k):
        to = lax.rem(me + k, n)
        return pltpu.make_async_remote_copy(
            src_ref=send2.at[to], dst_ref=recv2.at[me], send_sem=ss2.at[k],
            recv_sem=rs2.at[k], device_id={"chan": to}, device_id_type=MESH,
        )

    share = block // n

    def copy3(k):
        to = lax.rem(me + k, n)
        return pltpu.make_async_remote_copy(
            src_ref=send3.at[to], dst_ref=out_ref.at[0, pl.ds(me * share, share)],
            send_sem=ss3.at[k], recv_sem=rs3.at[k], device_id={"chan": to}, device_id_type=MESH,
        )

    for k in range(1, n):
        copy1(k).start()
    recv1[me] = send1[me]
    for k in range(1, n):
        copy1(k).wait_recv()
    total = recv1[0, :, :hc].astype(jnp.float32)
    for i in range(1, n):
        total = total + recv1[i, :, :hc].astype(jnp.float32)

    white = []
    for j in range(n):
        h, at = divmod(j * block, hc)
        part = total[h * mine : (h + 1) * mine, at : at + block]
        squares = part * part
        squares = squares + pltpu.roll(squares, mine // 2, 0)
        power = jnp.sum(squares, axis=1, keepdims=True) / (2 * block)
        white.append(part * lax.rsqrt(power + 1e-06))
    left = jnp.concatenate(white, axis=0).astype(jnp.bfloat16)
    weights = [recv1[i, :, hc:].astype(jnp.float32) for i in range(n)]
    rights = []
    for d in range(bands):
        pieces = []
        for i in range(n):
            if i + d + 1 < n:
                pieces.append(white[i + d + 1] * weights[i][d : d + 1, :])
            else:
                pieces.append(jnp.zeros((mine, block), jnp.float32))
        rights.append(jnp.concatenate(pieces, axis=0).astype(jnp.bfloat16))
    right = jnp.concatenate(rights, axis=1)
    stacks = lax.dot_general(
        left, right, (((0,), (0,)), ((), ())), preferred_element_type=jnp.float32
    )
    hb = bands // 2 * block
    stacks = jnp.concatenate(
        [stacks[:, :hb].reshape(n, share, hb), stacks[:, hb:].reshape(n, share, hb)], axis=1
    )
    send2[...] = stacks.astype(jnp.bfloat16)

    for k in range(1, n):
        copy2(k).start()
    recv2[me] = send2[me]
    for k in range(1, n):
        copy2(k).wait_recv()
    total = recv2[0].astype(jnp.float32)
    for i in range(1, n):
        total = total + recv2[i].astype(jnp.float32)
    total = total * (1.0 / (2 * bins))

    for to in range(n):
        chosen = jnp.zeros((share, block), jnp.float32)
        for d in range(bands):
            h, at = divmod(d * block, hb)
            owned = (owner_ref[d] == to).astype(jnp.float32)
            chosen = chosen + total[h * share : (h + 1) * share, at : at + block] * owned
        send3[to] = chosen
    for k in range(1, n):
        copy3(k).start()
    out_ref[0, pl.ds(me * share, share)] = send3[me]
    for k in range(1, n):
        copy3(k).wait_recv()
    for k in range(1, n):
        copy1(k).wait_send()
        copy2(k).wait_send()
        copy3(k).wait_send()


def fused(raw, taps, tile_dist, tile_count, owner):
    n = lax.axis_size("chan")
    rows, channels = raw.shape
    width = taps.shape[0]
    half = (width - 1) // 2
    bands = tile_dist.shape[1]
    block = channels // n
    steps = rows // 5
    mine = 2 * (steps * n // 16) // n
    lead = (128 - steps) // 2
    lanes = 1024
    start = lanes - 5 * lead - half
    line = jnp.pad(taps.astype(jnp.float32), (start, lanes - start - width))
    line = jnp.broadcast_to(line[None], (8, lanes))
    vmem, smem = pl.BlockSpec(memory_space=pltpu.VMEM), pl.BlockSpec(memory_space=pltpu.SMEM)
    share = block // n
    sems = [pltpu.SemaphoreType.DMA((n,)) for _ in range(6)]
    return pl.pallas_call(
        functools.partial(fused_kernel, n, width, bands),
        out_shape=jax.ShapeDtypeStruct((1, block, block), jnp.float32),
        in_specs=[smem, smem, smem, vmem, vmem],
        out_specs=vmem,
        scratch_shapes=[
            pltpu.VMEM((n, 2 * mine, channels // 2 + 128), jnp.bfloat16),
            pltpu.VMEM((n, 2 * mine, channels // 2 + 128), jnp.bfloat16),
            pltpu.VMEM((n, 2 * share, bands // 2 * block), jnp.bfloat16),
            pltpu.VMEM((n, 2 * share, bands // 2 * block), jnp.bfloat16),
            pltpu.VMEM((n, share, block), jnp.float32),
            *sems,
        ],
        compiler_params=pltpu.CompilerParams(
            collective_id=0, has_side_effects=True, vmem_limit_bytes=40 * 2**20
        ),
    )(tile_dist, tile_count, owner, raw, line)


def shards(raw, taps, tile_dist, tile_count, owner):
    n = lax.axis_size("chan")
    rows, channels = raw.shape
    steps = rows // 5
    fits = (
        channels == 128 * n
        and n == 16
        and rows == 320
        and taps.shape[0] == 255
        and tile_dist.shape[1] == 4
    )
    path = fused if fits else streamed
    return path(raw, taps, tile_dist, tile_count, owner)


def solution(mesh):
    in_specs = (P("chan", "groups"), P(), P("chan", "groups"), P(("groups", "chan")), P("groups"))
    out_specs = P("chan", "groups", None)
    return jax.shard_map(shards, mesh=mesh, in_specs=in_specs, out_specs=out_specs, check_vma=False)
```

```python
import functools
import math

import jax
import jax.numpy as jnp
from jax import lax
from jax.experimental import pallas as pl
from jax.experimental.pallas import tpu as pltpu
from jax.sharding import PartitionSpec as P

MESH = pl.DeviceIdType.MESH


def extended(x, sides, width):
    for axis, dim in sides:
        size, length = (lax.axis_size(axis), x.shape[dim])
        up = [(i, (i + 1) % size) for i in range(size - 1)]
        down = [(j, i) for i, j in up]
        last = lax.slice_in_dim(x, length - width, length, axis=dim)
        initial = lax.slice_in_dim(x, 0, width, axis=dim)
        before = lax.ppermute(last, axis, up)
        after = lax.ppermute(initial, axis, down)
        x = jnp.concatenate([before, x, after], axis=dim)
    return x


def passed_along(x, axis, by):
    size = lax.axis_size(axis)
    pairs = [(i, i + by) for i in range(size) if 0 <= i + by < size]
    return lax.ppermute(x, axis, pairs)


def band_matrix(taps, out_rows, in_cols):
    period = in_cols + 5
    padded = jnp.pad(taps, (0, period - taps.shape[0]))
    return jnp.tile(padded, out_rows)[: out_rows * in_cols].reshape(out_rows, in_cols)


def whiten(block):
    length, channels = block.shape
    bins = length // 16
    freqs = jnp.arange(1, bins + 1, dtype=jnp.int32)[:, None]
    times = jnp.arange(length, dtype=jnp.int32)[None, :]
    angle = (freqs * times % length).astype(jnp.float32) * (2.0 * math.pi / length)
    table = jnp.concatenate([jnp.cos(angle), -jnp.sin(angle)], axis=0)
    table_high = table.astype(jnp.bfloat16)
    table_low = (table - table_high.astype(jnp.float32)).astype(jnp.bfloat16)
    spectrum = jnp.dot(table_high, block, preferred_element_type=jnp.float32)
    spectrum = spectrum + jnp.dot(table_low, block, preferred_element_type=jnp.float32)
    squares = spectrum * spectrum
    power = jnp.sum(squares[:bins] + squares[bins:], axis=1) / (2 * channels)
    gain = lax.rsqrt(power + 1e-06)
    return (spectrum * jnp.concatenate([gain, gain])[:, None]).astype(jnp.bfloat16)


def cross_tile(mine, partner, scale):
    product = lax.dot_general(
        mine, partner, (((0,), (0,)), ((), ())), preferred_element_type=jnp.float32
    )
    return product * scale


def streamed(raw, taps, tile_dist, tile_count, owner):
    rows = raw.shape[0]
    width = taps.shape[0]
    half = (width - 1) // 2
    out_rows = rows // 5
    banded = band_matrix(taps, out_rows, rows + 2 * half)
    padded = extended(raw, (("chan", 0),), half)
    filtered = jnp.dot(banded, padded, preferred_element_type=jnp.float32)
    decimated = filtered.astype(jnp.bfloat16)
    regrouped = lax.all_to_all(decimated, "chan", split_axis=1, concat_axis=0, tiled=True)
    whitened = whiten(regrouped)
    channels = whitened.shape[1]
    scale = 1.0 / whitened.shape[0]
    bands = tile_dist.shape[1]
    slots = jnp.arange(bands, dtype=jnp.int32) < tile_count[0]
    stacks = []
    for distance in range(1, bands + 1):
        partner = passed_along(whitened, "chan", -distance)
        listed = jnp.sum(((tile_dist[0] == distance) & slots).astype(jnp.int32))
        tile = lax.cond(
            listed > 0,
            lambda first, second: cross_tile(first, second, scale),
            lambda first, second: jnp.zeros((channels, channels), jnp.float32),
            whitened,
            partner,
        )
        stacks.append(tile)
    stacked = jnp.stack(stacks)
    totals = lax.psum(stacked, "chan")
    selected = (owner == lax.axis_index("chan")).astype(jnp.float32)
    return jnp.einsum("b,bxy->xy", selected, totals, precision=lax.Precision.HIGHEST)[None]


def split(x):
    high = x.astype(jnp.bfloat16)
    low = (x - high.astype(jnp.float32)).astype(jnp.bfloat16)
    return high, low


def mm(a, b):
    return jnp.dot(a, b, preferred_element_type=jnp.float32)


def fused_kernel(
    n, width, bands,
    dist_ref, count_ref, owner_ref, raw_ref, taps_ref, out_ref,
    both, pair, send1, recv1, send2, recv2, send3, ss0, rs0, ss1, rs1, ss2, rs2, ss3, rs3,
):
    me = lax.axis_index("chan")
    chips = n // 2
    chip, core = me // 2, me % 2
    rows, channels = raw_ref.shape
    block = channels // n
    steps = rows // 5
    length = steps * n
    bins = length // 16
    mine = 2 * bins // n
    hc = channels // 2
    window = 128
    lead = (window - steps) // 2

    barrier = pltpu.get_barrier_semaphore()
    for k in range(1, n):
        pl.semaphore_signal(
            barrier, inc=1, device_id={"chan": lax.rem(me + k, n)}, device_id_type=MESH
        )

    lanes = taps_ref.shape[1]
    first = pltpu.roll(taps_ref[...], 0, 1, stride=5, stride_axis=0)
    banded = jnp.concatenate(
        [pltpu.roll(first, 40 * q, 1)[:, :384] for q in range(window // 8)], axis=0
    ).astype(jnp.bfloat16)[:, :rows]
    row = lax.broadcasted_iota(jnp.int32, (2 * bins, window), 0)
    col = lax.broadcasted_iota(jnp.int32, (2 * bins, window), 1)
    place = row % mine
    order = row // mine
    holder = (order % chips) * 2 + order // chips
    freq = holder * (mine // 2) + place % (mine // 2) + 1
    time = me * steps - lead + col
    turn = (freq * time + jnp.where(place >= mine // 2, length // 4, 0)) & (length - 1)
    table = jnp.cos(turn.astype(jnp.float32) * (2.0 * math.pi / length))
    table = jnp.where((time >= 0) & (time < length), table, 0.0)
    table_high, table_low = split(table)
    gmap = mm(table_high, banded) + mm(table_low, banded)
    gmap_high, gmap_low = split(gmap)

    chunk = 256
    for c in range(hc // chunk):
        halves = []
        for h in range(2):
            part = raw_ref[:, h * hc + c * chunk : h * hc + (c + 1) * chunk]
            spectra = mm(gmap_high, part) + mm(gmap_low, part)
            halves.append(spectra.reshape(n, mine, chunk))
        both[:, :, c * chunk : (c + 1) * chunk] = jnp.concatenate(halves, axis=1).astype(
            jnp.bfloat16
        )
    line = lax.broadcasted_iota(jnp.int32, (2 * mine, 128), 0)
    info = jnp.zeros((2 * mine, 128), jnp.float32)
    for d in range(bands):
        listed = jnp.int32(0)
        for s in range(bands):
            hit = (dist_ref[0, s] == d + 1) & (s < count_ref[0])
            listed = listed + hit.astype(jnp.int32)
        info = jnp.where(line == core * mine + d, listed.astype(jnp.float32), info)
    both[:, :, hc:] = jnp.broadcast_to(info[None], (n, 2 * mine, 128)).astype(jnp.bfloat16)

    pl.semaphore_wait(barrier, n - 1)

    first_copy = pltpu.make_async_remote_copy(
        src_ref=both.at[pl.ds((1 - core) * chips, chips)], dst_ref=pair, send_sem=ss0,
        recv_sem=rs0, device_id={"chan": chip * 2 + 1 - core}, device_id_type=MESH,
    )

    def copy1(k):
        to = lax.rem(chip + k, chips)
        return pltpu.make_async_remote_copy(
            src_ref=send1.at[to], dst_ref=recv1.at[chip], send_sem=ss1.at[k],
            recv_sem=rs1.at[k], device_id={"chan": to * 2 + core}, device_id_type=MESH,
        )

    def copy2(k):
        to = lax.rem(me + k, n)
        return pltpu.make_async_remote_copy(
            src_ref=send2.at[to], dst_ref=recv2.at[me], send_sem=ss2.at[k],
            recv_sem=rs2.at[k], device_id={"chan": to}, device_id_type=MESH,
        )

    share = block // n

    def copy3(k):
        to = lax.rem(me + k, n)
        return pltpu.make_async_remote_copy(
            src_ref=send3.at[to], dst_ref=out_ref.at[0, pl.ds(me * share, share)],
            send_sem=ss3.at[k], recv_sem=rs3.at[k], device_id={"chan": to}, device_id_type=MESH,
        )

    first_copy.start()
    first_copy.wait_recv()
    for k in range(1, chips):
        to = lax.rem(chip + k, chips)
        own = both[core * chips + to].astype(jnp.float32)
        send1[to] = (own + pair[to].astype(jnp.float32)).astype(jnp.bfloat16)
        copy1(k).start()
    own = both[core * chips + chip].astype(jnp.float32)
    recv1[chip] = (own + pair[chip].astype(jnp.float32)).astype(jnp.bfloat16)
    for k in range(1, chips):
        copy1(k).wait_recv()
    total = recv1[0, :, :hc].astype(jnp.float32)
    for i in range(1, chips):
        total = total + recv1[i, :, :hc].astype(jnp.float32)

    white = []
    for j in range(n):
        h, at = divmod(j * block, hc)
        part = total[h * mine : (h + 1) * mine, at : at + block]
        squares = part * part
        squares = squares + pltpu.roll(squares, mine // 2, 0)
        power = jnp.sum(squares, axis=1, keepdims=True) / (2 * block)
        white.append(part * lax.rsqrt(power + 1e-06))
    left = jnp.concatenate(white, axis=0).astype(jnp.bfloat16)
    weights = [recv1[i, :, hc:].astype(jnp.float32) for i in range(chips)]
    rights = []
    for d in range(bands):
        pieces = []
        for i in range(n):
            if i + d + 1 < n:
                pieces.append(white[i + d + 1] * weights[i // 2][i % 2 * mine + d : i % 2 * mine + d + 1, :])
            else:
                pieces.append(jnp.zeros((mine, block), jnp.float32))
        rights.append(jnp.concatenate(pieces, axis=0).astype(jnp.bfloat16))
    right = jnp.concatenate(rights, axis=1)
    stacks = lax.dot_general(
        left, right, (((0,), (0,)), ((), ())), preferred_element_type=jnp.float32
    )
    hb = bands // 2 * block
    stacks = jnp.concatenate(
        [stacks[:, :hb].reshape(n, share, hb), stacks[:, hb:].reshape(n, share, hb)], axis=1
    )
    send2[...] = stacks.astype(jnp.bfloat16)

    for k in range(1, n):
        copy2(k).start()
    recv2[me] = send2[me]
    for k in range(1, n):
        copy2(k).wait_recv()
    total = recv2[0].astype(jnp.float32)
    for i in range(1, n):
        total = total + recv2[i].astype(jnp.float32)
    total = total * (1.0 / (2 * bins))

    for to in range(n):
        chosen = jnp.zeros((share, block), jnp.float32)
        for d in range(bands):
            h, at = divmod(d * block, hb)
            owned = (owner_ref[d] == to).astype(jnp.float32)
            chosen = chosen + total[h * share : (h + 1) * share, at : at + block] * owned
        send3[to] = chosen
    for k in range(1, n):
        copy3(k).start()
    out_ref[0, pl.ds(me * share, share)] = send3[me]
    for k in range(1, n):
        copy3(k).wait_recv()
    first_copy.wait_send()
    for k in range(1, chips):
        copy1(k).wait_send()
    for k in range(1, n):
        copy2(k).wait_send()
        copy3(k).wait_send()


def fused(raw, taps, tile_dist, tile_count, owner):
    n = lax.axis_size("chan")
    rows, channels = raw.shape
    width = taps.shape[0]
    half = (width - 1) // 2
    bands = tile_dist.shape[1]
    block = channels // n
    steps = rows // 5
    mine = 2 * (steps * n // 16) // n
    lead = (128 - steps) // 2
    lanes = 1024
    start = lanes - 5 * lead - half
    line = jnp.pad(taps.astype(jnp.float32), (start, lanes - start - width))
    line = jnp.broadcast_to(line[None], (8, lanes))
    vmem, smem = pl.BlockSpec(memory_space=pltpu.VMEM), pl.BlockSpec(memory_space=pltpu.SMEM)
    share = block // n
    sems = [pltpu.SemaphoreType.DMA((n,)) for _ in range(6)]
    return pl.pallas_call(
        functools.partial(fused_kernel, n, width, bands),
        out_shape=jax.ShapeDtypeStruct((1, block, block), jnp.float32),
        in_specs=[smem, smem, smem, vmem, vmem],
        out_specs=vmem,
        scratch_shapes=[
            pltpu.VMEM((n, 2 * mine, channels // 2 + 128), jnp.bfloat16),
            pltpu.VMEM((n // 2, 2 * mine, channels // 2 + 128), jnp.bfloat16),
            pltpu.VMEM((n // 2, 2 * mine, channels // 2 + 128), jnp.bfloat16),
            pltpu.VMEM((n // 2, 2 * mine, channels // 2 + 128), jnp.bfloat16),
            pltpu.VMEM((n, 2 * share, bands // 2 * block), jnp.bfloat16),
            pltpu.VMEM((n, 2 * share, bands // 2 * block), jnp.bfloat16),
            pltpu.VMEM((n, share, block), jnp.float32),
            pltpu.SemaphoreType.DMA,
            pltpu.SemaphoreType.DMA,
            *sems,
        ],
        compiler_params=pltpu.CompilerParams(
            collective_id=0, has_side_effects=True, vmem_limit_bytes=40 * 2**20
        ),
    )(tile_dist, tile_count, owner, raw, line)


def shards(raw, taps, tile_dist, tile_count, owner):
    n = lax.axis_size("chan")
    rows, channels = raw.shape
    steps = rows // 5
    fits = (
        channels == 128 * n
        and n == 16
        and rows == 320
        and taps.shape[0] == 255
        and tile_dist.shape[1] == 4
    )
    path = fused if fits else streamed
    return path(raw, taps, tile_dist, tile_count, owner)


def solution(mesh):
    in_specs = (P("chan", "groups"), P(), P("chan", "groups"), P(("groups", "chan")), P("groups"))
    out_specs = P("chan", "groups", None)
    return jax.shard_map(shards, mesh=mesh, in_specs=in_specs, out_specs=out_specs, check_vma=False)
```

```python
import functools
import math

import jax
import jax.numpy as jnp
from jax import lax
from jax.experimental import pallas as pl
from jax.experimental.pallas import tpu as pltpu
from jax.sharding import PartitionSpec as P

MESH = pl.DeviceIdType.MESH


def extended(x, sides, width):
    for axis, dim in sides:
        size, length = (lax.axis_size(axis), x.shape[dim])
        up = [(i, (i + 1) % size) for i in range(size - 1)]
        down = [(j, i) for i, j in up]
        last = lax.slice_in_dim(x, length - width, length, axis=dim)
        initial = lax.slice_in_dim(x, 0, width, axis=dim)
        before = lax.ppermute(last, axis, up)
        after = lax.ppermute(initial, axis, down)
        x = jnp.concatenate([before, x, after], axis=dim)
    return x


def passed_along(x, axis, by):
    size = lax.axis_size(axis)
    pairs = [(i, i + by) for i in range(size) if 0 <= i + by < size]
    return lax.ppermute(x, axis, pairs)


def band_matrix(taps, out_rows, in_cols):
    period = in_cols + 5
    padded = jnp.pad(taps, (0, period - taps.shape[0]))
    return jnp.tile(padded, out_rows)[: out_rows * in_cols].reshape(out_rows, in_cols)


def whiten(block):
    length, channels = block.shape
    bins = length // 16
    freqs = jnp.arange(1, bins + 1, dtype=jnp.int32)[:, None]
    times = jnp.arange(length, dtype=jnp.int32)[None, :]
    angle = (freqs * times % length).astype(jnp.float32) * (2.0 * math.pi / length)
    table = jnp.concatenate([jnp.cos(angle), -jnp.sin(angle)], axis=0)
    table_high = table.astype(jnp.bfloat16)
    table_low = (table - table_high.astype(jnp.float32)).astype(jnp.bfloat16)
    spectrum = jnp.dot(table_high, block, preferred_element_type=jnp.float32)
    spectrum = spectrum + jnp.dot(table_low, block, preferred_element_type=jnp.float32)
    squares = spectrum * spectrum
    power = jnp.sum(squares[:bins] + squares[bins:], axis=1) / (2 * channels)
    gain = lax.rsqrt(power + 1e-06)
    return (spectrum * jnp.concatenate([gain, gain])[:, None]).astype(jnp.bfloat16)


def cross_tile(mine, partner, scale):
    product = lax.dot_general(
        mine, partner, (((0,), (0,)), ((), ())), preferred_element_type=jnp.float32
    )
    return product * scale


def streamed(raw, taps, tile_dist, tile_count, owner):
    rows = raw.shape[0]
    width = taps.shape[0]
    half = (width - 1) // 2
    out_rows = rows // 5
    banded = band_matrix(taps, out_rows, rows + 2 * half)
    padded = extended(raw, (("chan", 0),), half)
    filtered = jnp.dot(banded, padded, preferred_element_type=jnp.float32)
    decimated = filtered.astype(jnp.bfloat16)
    regrouped = lax.all_to_all(decimated, "chan", split_axis=1, concat_axis=0, tiled=True)
    whitened = whiten(regrouped)
    channels = whitened.shape[1]
    scale = 1.0 / whitened.shape[0]
    bands = tile_dist.shape[1]
    slots = jnp.arange(bands, dtype=jnp.int32) < tile_count[0]
    stacks = []
    for distance in range(1, bands + 1):
        partner = passed_along(whitened, "chan", -distance)
        listed = jnp.sum(((tile_dist[0] == distance) & slots).astype(jnp.int32))
        tile = lax.cond(
            listed > 0,
            lambda first, second: cross_tile(first, second, scale),
            lambda first, second: jnp.zeros((channels, channels), jnp.float32),
            whitened,
            partner,
        )
        stacks.append(tile)
    stacked = jnp.stack(stacks)
    totals = lax.psum(stacked, "chan")
    selected = (owner == lax.axis_index("chan")).astype(jnp.float32)
    return jnp.einsum("b,bxy->xy", selected, totals, precision=lax.Precision.HIGHEST)[None]


def split(x):
    high = x.astype(jnp.bfloat16)
    low = (x - high.astype(jnp.float32)).astype(jnp.bfloat16)
    return high, low


def mm(a, b):
    return jnp.dot(a, b, preferred_element_type=jnp.float32)


def fused_kernel(
    n, width, bands,
    dist_hbm, count_hbm, owner_hbm, raw_hbm, taps_ref, out_ref,
    dist_ref, count_ref, owner_ref, raw_ref, loads, both, pair, send1, recv1, both2, pair2, send2, recv2, send3, ss0, rs0, ss4, rs4, ss1, rs1, ss2, rs2, ss3, rs3,
):
    me = lax.axis_index("chan")
    chips = n // 2
    chip, core = me // 2, me % 2
    rows, channels = raw_ref.shape
    block = channels // n
    steps = rows // 5
    length = steps * n
    bins = length // 16
    mine = 2 * bins // n
    hc = channels // 2
    window = 128
    lead = (window - steps) // 2

    loaded = [
        pltpu.make_async_copy(source, held, loads.at[at])
        for at, (source, held) in enumerate(
            [
                (raw_hbm, raw_ref),
                (dist_hbm, dist_ref),
                (count_hbm, count_ref),
                (owner_hbm, owner_ref),
            ]
        )
    ]
    for load in loaded:
        load.start()
    barrier = pltpu.get_barrier_semaphore()
    for k in range(1, n):
        pl.semaphore_signal(
            barrier, inc=1, device_id={"chan": lax.rem(me + k, n)}, device_id_type=MESH
        )

    lanes = taps_ref.shape[1]
    first = pltpu.roll(taps_ref[...], 0, 1, stride=5, stride_axis=0)
    banded = jnp.concatenate(
        [pltpu.roll(first, 40 * q, 1)[:, :384] for q in range(window // 8)], axis=0
    ).astype(jnp.bfloat16)[:, :rows]
    row = lax.broadcasted_iota(jnp.int32, (2 * bins, window), 0)
    col = lax.broadcasted_iota(jnp.int32, (2 * bins, window), 1)
    place = row % mine
    order = row // mine
    holder = (order % chips) * 2 + order // chips
    freq = holder * (mine // 2) + place % (mine // 2) + 1
    time = me * steps - lead + col
    turn = (freq * time + jnp.where(place >= mine // 2, length // 4, 0)) & (length - 1)
    table = jnp.cos(turn.astype(jnp.float32) * (2.0 * math.pi / length))
    table = jnp.where((time >= 0) & (time < length), table, 0.0)
    table_high, table_low = split(table)
    gmap = mm(table_high, banded) + mm(table_low, banded)
    gmap_high, gmap_low = split(gmap)

    for load in loaded:
        load.wait()
    chunk = 256
    for c in range(hc // chunk):
        halves = []
        for h in range(2):
            part = raw_ref[:, h * hc + c * chunk : h * hc + (c + 1) * chunk]
            spectra = mm(gmap_high, part) + mm(gmap_low, part)
            halves.append(spectra.reshape(n, mine, chunk))
        both[:, :, c * chunk : (c + 1) * chunk] = jnp.concatenate(halves, axis=1).astype(
            jnp.bfloat16
        )
    line = lax.broadcasted_iota(jnp.int32, (2 * mine, 128), 0)
    info = jnp.zeros((2 * mine, 128), jnp.float32)
    for d in range(bands):
        listed = jnp.int32(0)
        for s in range(bands):
            hit = (dist_ref[0, s] == d + 1) & (s < count_ref[0])
            listed = listed + hit.astype(jnp.int32)
        info = jnp.where(line == core * mine + d, listed.astype(jnp.float32), info)
    both[:, :, hc:] = jnp.broadcast_to(info[None], (n, 2 * mine, 128)).astype(jnp.bfloat16)

    pl.semaphore_wait(barrier, n - 1)

    first_copy = pltpu.make_async_remote_copy(
        src_ref=both.at[pl.ds((1 - core) * chips, chips)], dst_ref=pair, send_sem=ss0,
        recv_sem=rs0, device_id={"chan": chip * 2 + 1 - core}, device_id_type=MESH,
    )

    def copy1(k):
        to = lax.rem(chip + k, chips)
        return pltpu.make_async_remote_copy(
            src_ref=send1.at[to], dst_ref=recv1.at[chip], send_sem=ss1.at[k],
            recv_sem=rs1.at[k], device_id={"chan": to * 2 + core}, device_id_type=MESH,
        )

    second_copy = pltpu.make_async_remote_copy(
        src_ref=both2.at[pl.ds((1 - core) * chips, chips)], dst_ref=pair2, send_sem=ss4,
        recv_sem=rs4, device_id={"chan": chip * 2 + 1 - core}, device_id_type=MESH,
    )

    def copy2(k):
        to = lax.rem(chip + k, chips)
        return pltpu.make_async_remote_copy(
            src_ref=send2.at[to], dst_ref=recv2.at[chip], send_sem=ss2.at[k],
            recv_sem=rs2.at[k], device_id={"chan": to * 2 + core}, device_id_type=MESH,
        )

    share = block // n
    place = (core * chips + chip) * share

    def copy3(k):
        to = lax.rem(me + k, n)
        return pltpu.make_async_remote_copy(
            src_ref=send3.at[to], dst_ref=out_ref.at[0, pl.ds(place, share)],
            send_sem=ss3.at[k], recv_sem=rs3.at[k], device_id={"chan": to}, device_id_type=MESH,
        )

    first_copy.start()
    first_copy.wait_recv()
    for k in range(1, chips):
        to = lax.rem(chip + k, chips)
        own = both[core * chips + to].astype(jnp.float32)
        send1[to] = (own + pair[to].astype(jnp.float32)).astype(jnp.bfloat16)
        copy1(k).start()
    own = both[core * chips + chip].astype(jnp.float32)
    recv1[chip] = (own + pair[chip].astype(jnp.float32)).astype(jnp.bfloat16)
    for k in range(1, chips):
        copy1(k).wait_recv()
    total = recv1[0, :, :hc].astype(jnp.float32)
    for i in range(1, chips):
        total = total + recv1[i, :, :hc].astype(jnp.float32)

    white = []
    for j in range(n):
        h, at = divmod(j * block, hc)
        part = total[h * mine : (h + 1) * mine, at : at + block]
        squares = part * part
        squares = squares + pltpu.roll(squares, mine // 2, 0)
        power = jnp.sum(squares, axis=1, keepdims=True) / (2 * block)
        white.append(part * lax.rsqrt(power + 1e-06))
    left = jnp.concatenate(white, axis=0).astype(jnp.bfloat16)
    weights = [recv1[i, :, hc:].astype(jnp.float32) for i in range(chips)]
    rights = []
    for d in range(bands):
        pieces = []
        for i in range(n):
            if i + d + 1 < n:
                pieces.append(white[i + d + 1] * weights[i // 2][i % 2 * mine + d : i % 2 * mine + d + 1, :])
            else:
                pieces.append(jnp.zeros((mine, block), jnp.float32))
        rights.append(jnp.concatenate(pieces, axis=0).astype(jnp.bfloat16))
    right = jnp.concatenate(rights, axis=1)
    stacks = lax.dot_general(
        left, right, (((0,), (0,)), ((), ())), preferred_element_type=jnp.float32
    )
    hb = bands // 2 * block
    stacks = jnp.concatenate(
        [stacks[:, :hb].reshape(n, share, hb), stacks[:, hb:].reshape(n, share, hb)], axis=1
    )
    both2[...] = stacks.astype(jnp.bfloat16)

    second_copy.start()
    second_copy.wait_recv()
    for k in range(1, chips):
        to = lax.rem(chip + k, chips)
        own = both2[core * chips + to].astype(jnp.float32)
        send2[to] = (own + pair2[to].astype(jnp.float32)).astype(jnp.bfloat16)
        copy2(k).start()
    own = both2[core * chips + chip].astype(jnp.float32)
    recv2[chip] = (own + pair2[chip].astype(jnp.float32)).astype(jnp.bfloat16)
    for k in range(1, chips):
        copy2(k).wait_recv()
    total = recv2[0].astype(jnp.float32)
    for i in range(1, chips):
        total = total + recv2[i].astype(jnp.float32)
    total = total * (1.0 / (2 * bins))

    for to in range(n):
        chosen = jnp.zeros((share, block), jnp.float32)
        for d in range(bands):
            h, at = divmod(d * block, hb)
            owned = (owner_ref[d] == to).astype(jnp.float32)
            chosen = chosen + total[h * share : (h + 1) * share, at : at + block] * owned
        send3[to] = chosen
    for k in range(1, n):
        copy3(k).start()
    out_ref[0, pl.ds(place, share)] = send3[me]
    for k in range(1, n):
        copy3(k).wait_recv()
    first_copy.wait_send()
    for k in range(1, chips):
        copy1(k).wait_send()
    second_copy.wait_send()
    for k in range(1, chips):
        copy2(k).wait_send()
    for k in range(1, n):
        copy3(k).wait_send()


def fused(raw, taps, tile_dist, tile_count, owner):
    n = lax.axis_size("chan")
    rows, channels = raw.shape
    width = taps.shape[0]
    half = (width - 1) // 2
    bands = tile_dist.shape[1]
    block = channels // n
    steps = rows // 5
    mine = 2 * (steps * n // 16) // n
    lead = (128 - steps) // 2
    lanes = 1024
    start = lanes - 5 * lead - half
    line = jnp.pad(taps.astype(jnp.float32), (start, lanes - start - width))
    line = jnp.broadcast_to(line[None], (8, lanes))
    vmem, hbm = pl.BlockSpec(memory_space=pltpu.VMEM), pl.BlockSpec(memory_space=pltpu.HBM)
    share = block // n
    sems = [pltpu.SemaphoreType.DMA((n,)) for _ in range(6)]
    return pl.pallas_call(
        functools.partial(fused_kernel, n, width, bands),
        out_shape=jax.ShapeDtypeStruct((1, block, block), jnp.float32),
        in_specs=[hbm, hbm, hbm, hbm, vmem],
        out_specs=vmem,
        scratch_shapes=[
            pltpu.SMEM(tile_dist.shape, jnp.int32),
            pltpu.SMEM(tile_count.shape, jnp.int32),
            pltpu.SMEM(owner.shape, jnp.int32),
            pltpu.VMEM(raw.shape, raw.dtype),
            pltpu.SemaphoreType.DMA((4,)),
            pltpu.VMEM((n, 2 * mine, channels // 2 + 128), jnp.bfloat16),
            pltpu.VMEM((n // 2, 2 * mine, channels // 2 + 128), jnp.bfloat16),
            pltpu.VMEM((n // 2, 2 * mine, channels // 2 + 128), jnp.bfloat16),
            pltpu.VMEM((n // 2, 2 * mine, channels // 2 + 128), jnp.bfloat16),
            pltpu.VMEM((n, 2 * share, bands // 2 * block), jnp.bfloat16),
            pltpu.VMEM((n // 2, 2 * share, bands // 2 * block), jnp.bfloat16),
            pltpu.VMEM((n // 2, 2 * share, bands // 2 * block), jnp.bfloat16),
            pltpu.VMEM((n // 2, 2 * share, bands // 2 * block), jnp.bfloat16),
            pltpu.VMEM((n, share, block), jnp.float32),
            *[pltpu.SemaphoreType.DMA] * 4,
            *sems,
        ],
        compiler_params=pltpu.CompilerParams(
            collective_id=0, has_side_effects=True, vmem_limit_bytes=61 * 2**20
        ),
    )(tile_dist, tile_count, owner, raw, line)


def shards(raw, taps, tile_dist, tile_count, owner):
    n = lax.axis_size("chan")
    rows, channels = raw.shape
    steps = rows // 5
    fits = (
        channels == 128 * n
        and n == 16
        and rows == 320
        and taps.shape[0] == 255
        and tile_dist.shape[1] == 4
    )
    path = fused if fits else streamed
    return path(raw, taps, tile_dist, tile_count, owner)


def solution(mesh):
    in_specs = (P("chan", "groups"), P(), P("chan", "groups"), P(("groups", "chan")), P("groups"))
    out_specs = P("chan", "groups", None)
    return jax.shard_map(shards, mesh=mesh, in_specs=in_specs, out_specs=out_specs, check_vma=False)
```

```python
import functools
import math

import jax
import jax.numpy as jnp
from jax import lax
from jax.experimental import pallas as pl
from jax.experimental.pallas import tpu as pltpu
from jax.sharding import PartitionSpec as P

MESH = pl.DeviceIdType.MESH


def extended(x, sides, width):
    for axis, dim in sides:
        size, length = (lax.axis_size(axis), x.shape[dim])
        up = [(i, (i + 1) % size) for i in range(size - 1)]
        down = [(j, i) for i, j in up]
        last = lax.slice_in_dim(x, length - width, length, axis=dim)
        initial = lax.slice_in_dim(x, 0, width, axis=dim)
        before = lax.ppermute(last, axis, up)
        after = lax.ppermute(initial, axis, down)
        x = jnp.concatenate([before, x, after], axis=dim)
    return x


def passed_along(x, axis, by):
    size = lax.axis_size(axis)
    pairs = [(i, i + by) for i in range(size) if 0 <= i + by < size]
    return lax.ppermute(x, axis, pairs)


def band_matrix(taps, out_rows, in_cols):
    period = in_cols + 5
    padded = jnp.pad(taps, (0, period - taps.shape[0]))
    return jnp.tile(padded, out_rows)[: out_rows * in_cols].reshape(out_rows, in_cols)


def whiten(block):
    length, channels = block.shape
    bins = length // 16
    freqs = jnp.arange(1, bins + 1, dtype=jnp.int32)[:, None]
    times = jnp.arange(length, dtype=jnp.int32)[None, :]
    angle = (freqs * times % length).astype(jnp.float32) * (2.0 * math.pi / length)
    table = jnp.concatenate([jnp.cos(angle), -jnp.sin(angle)], axis=0)
    table_high = table.astype(jnp.bfloat16)
    table_low = (table - table_high.astype(jnp.float32)).astype(jnp.bfloat16)
    spectrum = jnp.dot(table_high, block, preferred_element_type=jnp.float32)
    spectrum = spectrum + jnp.dot(table_low, block, preferred_element_type=jnp.float32)
    squares = spectrum * spectrum
    power = jnp.sum(squares[:bins] + squares[bins:], axis=1) / (2 * channels)
    gain = lax.rsqrt(power + 1e-06)
    return (spectrum * jnp.concatenate([gain, gain])[:, None]).astype(jnp.bfloat16)


def cross_tile(mine, partner, scale):
    product = lax.dot_general(
        mine, partner, (((0,), (0,)), ((), ())), preferred_element_type=jnp.float32
    )
    return product * scale


def streamed(raw, taps, tile_dist, tile_count, owner):
    rows = raw.shape[0]
    width = taps.shape[0]
    half = (width - 1) // 2
    out_rows = rows // 5
    banded = band_matrix(taps, out_rows, rows + 2 * half)
    padded = extended(raw, (("chan", 0),), half)
    filtered = jnp.dot(banded, padded, preferred_element_type=jnp.float32)
    decimated = filtered.astype(jnp.bfloat16)
    regrouped = lax.all_to_all(decimated, "chan", split_axis=1, concat_axis=0, tiled=True)
    whitened = whiten(regrouped)
    channels = whitened.shape[1]
    scale = 1.0 / whitened.shape[0]
    bands = tile_dist.shape[1]
    slots = jnp.arange(bands, dtype=jnp.int32) < tile_count[0]
    stacks = []
    for distance in range(1, bands + 1):
        partner = passed_along(whitened, "chan", -distance)
        listed = jnp.sum(((tile_dist[0] == distance) & slots).astype(jnp.int32))
        tile = lax.cond(
            listed > 0,
            lambda first, second: cross_tile(first, second, scale),
            lambda first, second: jnp.zeros((channels, channels), jnp.float32),
            whitened,
            partner,
        )
        stacks.append(tile)
    stacked = jnp.stack(stacks)
    totals = lax.psum(stacked, "chan")
    selected = (owner == lax.axis_index("chan")).astype(jnp.float32)
    return jnp.einsum("b,bxy->xy", selected, totals, precision=lax.Precision.HIGHEST)[None]


def split(x):
    high = x.astype(jnp.bfloat16)
    low = (x - high.astype(jnp.float32)).astype(jnp.bfloat16)
    return high, low


def mm(a, b):
    return jnp.dot(a, b, preferred_element_type=jnp.float32)


def fused_kernel(
    n, width, bands,
    dist_hbm, count_hbm, owner_hbm, raw_hbm, taps_ref, out_ref,
    dist_ref, count_ref, owner_ref, raw_ref, loads, both, pair, send1, recv1, both2, pair2, send2, recv2, send3, ss0, rs0, ss4, rs4, ss1, rs1, ss2, rs2, ss3, rs3,
):
    me = lax.axis_index("chan")
    chips = n // 2
    chip, core = me // 2, me % 2
    rows, channels = raw_ref.shape
    block = channels // n
    steps = rows // 5
    length = steps * n
    bins = length // 16
    mine = 2 * bins // n
    hc = channels // 2
    window = 128
    lead = (window - steps) // 2

    loaded = [
        pltpu.make_async_copy(source, held, loads.at[at])
        for at, (source, held) in enumerate(
            [
                (raw_hbm, raw_ref),
                (dist_hbm, dist_ref),
                (count_hbm, count_ref),
                (owner_hbm, owner_ref),
            ]
        )
    ]
    for load in loaded:
        load.start()
    barrier = pltpu.get_barrier_semaphore()
    for k in range(1, n):
        pl.semaphore_signal(
            barrier, inc=1, device_id={"chan": lax.rem(me + k, n)}, device_id_type=MESH
        )

    lanes = taps_ref.shape[1]
    first = pltpu.roll(taps_ref[...], 0, 1, stride=5, stride_axis=0)
    banded = jnp.concatenate(
        [pltpu.roll(first, 40 * q, 1)[:, :384] for q in range(window // 8)], axis=0
    ).astype(jnp.bfloat16)[:, :rows]
    row = lax.broadcasted_iota(jnp.int32, (2 * bins, window), 0)
    col = lax.broadcasted_iota(jnp.int32, (2 * bins, window), 1)
    place = row % mine
    order = row // mine
    holder = (order % chips) * 2 + order // chips
    freq = holder * (mine // 2) + place % (mine // 2) + 1
    time = me * steps - lead + col
    turn = (freq * time + jnp.where(place >= mine // 2, length // 4, 0)) & (length - 1)
    table = jnp.cos(turn.astype(jnp.float32) * (2.0 * math.pi / length))
    table = jnp.where((time >= 0) & (time < length), table, 0.0)
    table_high, table_low = split(table)
    gmap = mm(table_high, banded) + mm(table_low, banded)
    gmap_high, gmap_low = split(gmap)

    for load in loaded:
        load.wait()
    chunk = 256

    def transform(c):
        halves = []
        for h in range(2):
            part = raw_ref[:, h * hc + c * chunk : h * hc + (c + 1) * chunk]
            spectra = mm(gmap_high, part) + mm(gmap_low, part)
            halves.append(spectra.reshape(n, mine, chunk))
        both[:, :, c * chunk : (c + 1) * chunk] = jnp.concatenate(halves, axis=1).astype(
            jnp.bfloat16
        )

    pieces = [(0, hc // 2), (hc // 2, hc // 2 + 128)]
    for c in range(hc // chunk // 2):
        transform(c)
    line = lax.broadcasted_iota(jnp.int32, (2 * mine, 128), 0)
    info = jnp.zeros((2 * mine, 128), jnp.float32)
    for d in range(bands):
        listed = jnp.int32(0)
        for s in range(bands):
            hit = (dist_ref[0, s] == d + 1) & (s < count_ref[0])
            listed = listed + hit.astype(jnp.int32)
        info = jnp.where(line == core * mine + d, listed.astype(jnp.float32), info)
    both[:, :, hc:] = jnp.broadcast_to(info[None], (n, 2 * mine, 128)).astype(jnp.bfloat16)

    pl.semaphore_wait(barrier, n - 1)

    def copy0(p):
        cols = pl.ds(*pieces[p])
        return pltpu.make_async_remote_copy(
            src_ref=both.at[pl.ds((1 - core) * chips, chips), :, cols],
            dst_ref=pair.at[:, :, cols], send_sem=ss0.at[p], recv_sem=rs0.at[p],
            device_id={"chan": chip * 2 + 1 - core}, device_id_type=MESH,
        )

    def copy1(p, k):
        to = lax.rem(chip + k, chips)
        cols = pl.ds(*pieces[p])
        return pltpu.make_async_remote_copy(
            src_ref=send1.at[to, :, cols], dst_ref=recv1.at[chip, :, cols],
            send_sem=ss1.at[p * chips + k], recv_sem=rs1.at[p * chips + k],
            device_id={"chan": to * 2 + core}, device_id_type=MESH,
        )

    second_copy = pltpu.make_async_remote_copy(
        src_ref=both2.at[pl.ds((1 - core) * chips, chips)], dst_ref=pair2, send_sem=ss4,
        recv_sem=rs4, device_id={"chan": chip * 2 + 1 - core}, device_id_type=MESH,
    )

    def copy2(k):
        to = lax.rem(chip + k, chips)
        return pltpu.make_async_remote_copy(
            src_ref=send2.at[to], dst_ref=recv2.at[chip], send_sem=ss2.at[k],
            recv_sem=rs2.at[k], device_id={"chan": to * 2 + core}, device_id_type=MESH,
        )

    share = block // n
    place = (core * chips + chip) * share

    def copy3(k):
        to = lax.rem(me + k, n)
        return pltpu.make_async_remote_copy(
            src_ref=send3.at[to], dst_ref=out_ref.at[0, pl.ds(place, share)],
            send_sem=ss3.at[k], recv_sem=rs3.at[k], device_id={"chan": to}, device_id_type=MESH,
        )

    copy0(0).start()
    for c in range(hc // chunk // 2, hc // chunk):
        transform(c)
    copy0(1).start()
    for p in range(2):
        cols = slice(pieces[p][0], sum(pieces[p]))
        copy0(p).wait_recv()
        for k in range(1, chips):
            to = lax.rem(chip + k, chips)
            own = both[core * chips + to, :, cols].astype(jnp.float32)
            send1[to, :, cols] = (own + pair[to, :, cols].astype(jnp.float32)).astype(jnp.bfloat16)
            copy1(p, k).start()
        own = both[core * chips + chip, :, cols].astype(jnp.float32)
        recv1[chip, :, cols] = (own + pair[chip, :, cols].astype(jnp.float32)).astype(jnp.bfloat16)
    for p in range(2):
        for k in range(1, chips):
            copy1(p, k).wait_recv()
    total = recv1[0, :, :hc].astype(jnp.float32)
    for i in range(1, chips):
        total = total + recv1[i, :, :hc].astype(jnp.float32)

    white = []
    for j in range(n):
        h, at = divmod(j * block, hc)
        part = total[h * mine : (h + 1) * mine, at : at + block]
        squares = part * part
        squares = squares + pltpu.roll(squares, mine // 2, 0)
        power = jnp.sum(squares, axis=1, keepdims=True) / (2 * block)
        white.append(part * lax.rsqrt(power + 1e-06))
    left = jnp.concatenate(white, axis=0).astype(jnp.bfloat16)
    weights = [recv1[i, :, hc:].astype(jnp.float32) for i in range(chips)]
    rights = []
    for d in range(bands):
        tiles = []
        for i in range(n):
            if i + d + 1 < n:
                tiles.append(white[i + d + 1] * weights[i // 2][i % 2 * mine + d : i % 2 * mine + d + 1, :])
            else:
                tiles.append(jnp.zeros((mine, block), jnp.float32))
        rights.append(jnp.concatenate(tiles, axis=0).astype(jnp.bfloat16))
    right = jnp.concatenate(rights, axis=1)
    stacks = lax.dot_general(
        left, right, (((0,), (0,)), ((), ())), preferred_element_type=jnp.float32
    )
    hb = bands // 2 * block
    stacks = jnp.concatenate(
        [stacks[:, :hb].reshape(n, share, hb), stacks[:, hb:].reshape(n, share, hb)], axis=1
    )
    both2[...] = stacks.astype(jnp.bfloat16)

    second_copy.start()
    second_copy.wait_recv()
    for k in range(1, chips):
        to = lax.rem(chip + k, chips)
        own = both2[core * chips + to].astype(jnp.float32)
        send2[to] = (own + pair2[to].astype(jnp.float32)).astype(jnp.bfloat16)
        copy2(k).start()
    own = both2[core * chips + chip].astype(jnp.float32)
    recv2[chip] = (own + pair2[chip].astype(jnp.float32)).astype(jnp.bfloat16)
    for k in range(1, chips):
        copy2(k).wait_recv()
    total = recv2[0].astype(jnp.float32)
    for i in range(1, chips):
        total = total + recv2[i].astype(jnp.float32)
    total = total * (1.0 / (2 * bins))

    for to in range(n):
        chosen = jnp.zeros((share, block), jnp.float32)
        for d in range(bands):
            h, at = divmod(d * block, hb)
            owned = (owner_ref[d] == to).astype(jnp.float32)
            chosen = chosen + total[h * share : (h + 1) * share, at : at + block] * owned
        send3[to] = chosen
    for k in range(1, n):
        copy3(k).start()
    out_ref[0, pl.ds(place, share)] = send3[me]
    for k in range(1, n):
        copy3(k).wait_recv()
    for p in range(2):
        copy0(p).wait_send()
        for k in range(1, chips):
            copy1(p, k).wait_send()
    second_copy.wait_send()
    for k in range(1, chips):
        copy2(k).wait_send()
    for k in range(1, n):
        copy3(k).wait_send()


def fused(raw, taps, tile_dist, tile_count, owner):
    n = lax.axis_size("chan")
    rows, channels = raw.shape
    width = taps.shape[0]
    half = (width - 1) // 2
    bands = tile_dist.shape[1]
    block = channels // n
    steps = rows // 5
    mine = 2 * (steps * n // 16) // n
    lead = (128 - steps) // 2
    lanes = 1024
    start = lanes - 5 * lead - half
    line = jnp.pad(taps.astype(jnp.float32), (start, lanes - start - width))
    line = jnp.broadcast_to(line[None], (8, lanes))
    vmem, hbm = pl.BlockSpec(memory_space=pltpu.VMEM), pl.BlockSpec(memory_space=pltpu.HBM)
    share = block // n
    sems = [pltpu.SemaphoreType.DMA((n,)) for _ in range(6)]
    return pl.pallas_call(
        functools.partial(fused_kernel, n, width, bands),
        out_shape=jax.ShapeDtypeStruct((1, block, block), jnp.float32),
        in_specs=[hbm, hbm, hbm, hbm, vmem],
        out_specs=vmem,
        scratch_shapes=[
            pltpu.SMEM(tile_dist.shape, jnp.int32),
            pltpu.SMEM(tile_count.shape, jnp.int32),
            pltpu.SMEM(owner.shape, jnp.int32),
            pltpu.VMEM(raw.shape, raw.dtype),
            pltpu.SemaphoreType.DMA((4,)),
            pltpu.VMEM((n, 2 * mine, channels // 2 + 128), jnp.bfloat16),
            pltpu.VMEM((n // 2, 2 * mine, channels // 2 + 128), jnp.bfloat16),
            pltpu.VMEM((n // 2, 2 * mine, channels // 2 + 128), jnp.bfloat16),
            pltpu.VMEM((n // 2, 2 * mine, channels // 2 + 128), jnp.bfloat16),
            pltpu.VMEM((n, 2 * share, bands // 2 * block), jnp.bfloat16),
            pltpu.VMEM((n // 2, 2 * share, bands // 2 * block), jnp.bfloat16),
            pltpu.VMEM((n // 2, 2 * share, bands // 2 * block), jnp.bfloat16),
            pltpu.VMEM((n // 2, 2 * share, bands // 2 * block), jnp.bfloat16),
            pltpu.VMEM((n, share, block), jnp.float32),
            pltpu.SemaphoreType.DMA((2,)),
            pltpu.SemaphoreType.DMA((2,)),
            pltpu.SemaphoreType.DMA,
            pltpu.SemaphoreType.DMA,
            *sems,
        ],
        compiler_params=pltpu.CompilerParams(
            collective_id=0, has_side_effects=True, vmem_limit_bytes=61 * 2**20
        ),
    )(tile_dist, tile_count, owner, raw, line)


def shards(raw, taps, tile_dist, tile_count, owner):
    n = lax.axis_size("chan")
    rows, channels = raw.shape
    steps = rows // 5
    fits = (
        channels == 128 * n
        and n == 16
        and rows == 320
        and taps.shape[0] == 255
        and tile_dist.shape[1] == 4
    )
    path = fused if fits else streamed
    return path(raw, taps, tile_dist, tile_count, owner)


def solution(mesh):
    in_specs = (P("chan", "groups"), P(), P("chan", "groups"), P(("groups", "chan")), P("groups"))
    out_specs = P("chan", "groups", None)
    return jax.shard_map(shards, mesh=mesh, in_specs=in_specs, out_specs=out_specs, check_vma=False)
```

```python
import functools
import math

import jax
import jax.numpy as jnp
from jax import lax
from jax.experimental import pallas as pl
from jax.experimental.pallas import tpu as pltpu
from jax.sharding import PartitionSpec as P

MESH = pl.DeviceIdType.MESH


def extended(x, sides, width):
    for axis, dim in sides:
        size, length = (lax.axis_size(axis), x.shape[dim])
        up = [(i, (i + 1) % size) for i in range(size - 1)]
        down = [(j, i) for i, j in up]
        last = lax.slice_in_dim(x, length - width, length, axis=dim)
        initial = lax.slice_in_dim(x, 0, width, axis=dim)
        before = lax.ppermute(last, axis, up)
        after = lax.ppermute(initial, axis, down)
        x = jnp.concatenate([before, x, after], axis=dim)
    return x


def passed_along(x, axis, by):
    size = lax.axis_size(axis)
    pairs = [(i, i + by) for i in range(size) if 0 <= i + by < size]
    return lax.ppermute(x, axis, pairs)


def band_matrix(taps, out_rows, in_cols):
    period = in_cols + 5
    padded = jnp.pad(taps, (0, period - taps.shape[0]))
    return jnp.tile(padded, out_rows)[: out_rows * in_cols].reshape(out_rows, in_cols)


def whiten(block):
    length, channels = block.shape
    bins = length // 16
    freqs = jnp.arange(1, bins + 1, dtype=jnp.int32)[:, None]
    times = jnp.arange(length, dtype=jnp.int32)[None, :]
    angle = (freqs * times % length).astype(jnp.float32) * (2.0 * math.pi / length)
    table = jnp.concatenate([jnp.cos(angle), -jnp.sin(angle)], axis=0)
    table_high = table.astype(jnp.bfloat16)
    table_low = (table - table_high.astype(jnp.float32)).astype(jnp.bfloat16)
    spectrum = jnp.dot(table_high, block, preferred_element_type=jnp.float32)
    spectrum = spectrum + jnp.dot(table_low, block, preferred_element_type=jnp.float32)
    squares = spectrum * spectrum
    power = jnp.sum(squares[:bins] + squares[bins:], axis=1) / (2 * channels)
    gain = lax.rsqrt(power + 1e-06)
    return (spectrum * jnp.concatenate([gain, gain])[:, None]).astype(jnp.bfloat16)


def cross_tile(mine, partner, scale):
    product = lax.dot_general(
        mine, partner, (((0,), (0,)), ((), ())), preferred_element_type=jnp.float32
    )
    return product * scale


def streamed(raw, taps, tile_dist, tile_count, owner):
    rows = raw.shape[0]
    width = taps.shape[0]
    half = (width - 1) // 2
    out_rows = rows // 5
    banded = band_matrix(taps, out_rows, rows + 2 * half)
    padded = extended(raw, (("chan", 0),), half)
    filtered = jnp.dot(banded, padded, preferred_element_type=jnp.float32)
    decimated = filtered.astype(jnp.bfloat16)
    regrouped = lax.all_to_all(decimated, "chan", split_axis=1, concat_axis=0, tiled=True)
    whitened = whiten(regrouped)
    channels = whitened.shape[1]
    scale = 1.0 / whitened.shape[0]
    bands = tile_dist.shape[1]
    slots = jnp.arange(bands, dtype=jnp.int32) < tile_count[0]
    stacks = []
    for distance in range(1, bands + 1):
        partner = passed_along(whitened, "chan", -distance)
        listed = jnp.sum(((tile_dist[0] == distance) & slots).astype(jnp.int32))
        tile = lax.cond(
            listed > 0,
            lambda first, second: cross_tile(first, second, scale),
            lambda first, second: jnp.zeros((channels, channels), jnp.float32),
            whitened,
            partner,
        )
        stacks.append(tile)
    stacked = jnp.stack(stacks)
    totals = lax.psum(stacked, "chan")
    selected = (owner == lax.axis_index("chan")).astype(jnp.float32)
    return jnp.einsum("b,bxy->xy", selected, totals, precision=lax.Precision.HIGHEST)[None]


def split(x):
    high = x.astype(jnp.bfloat16)
    low = (x - high.astype(jnp.float32)).astype(jnp.bfloat16)
    return high, low


def mm(a, b):
    return jnp.dot(a, b, preferred_element_type=jnp.float32)


def fused_kernel(
    n, width, bands,
    plan_hbm, raw_hbm, taps_ref, out_ref,
    plan_ref, raw_ref, loads, both, pair, send1, recv1, both2, pair2, send2, recv2, send3, ss0, rs0, ss4, rs4, ss1, rs1, ss2, rs2, ss3, rs3,
):
    me = lax.axis_index("chan")
    chips = n // 2
    chip, core = me // 2, me % 2
    rows, channels = raw_ref.shape
    block = channels // n
    steps = rows // 5
    length = steps * n
    bins = length // 16
    mine = 2 * bins // n
    hc = channels // 2
    window = 128
    lead = (window - steps) // 2

    loaded = [
        pltpu.make_async_copy(source, held, loads.at[at])
        for at, (source, held) in enumerate(
            [
                (raw_hbm, raw_ref),
                (plan_hbm, plan_ref),
            ]
        )
    ]
    for load in loaded:
        load.start()
    barrier = pltpu.get_barrier_semaphore()
    for k in range(1, n):
        pl.semaphore_signal(
            barrier, inc=1, device_id={"chan": lax.rem(me + k, n)}, device_id_type=MESH
        )

    lanes = taps_ref.shape[1]
    taps = jnp.broadcast_to(taps_ref[...], (8, taps_ref.shape[1]))
    first = pltpu.roll(taps, 0, 1, stride=5, stride_axis=0)
    banded = jnp.concatenate(
        [pltpu.roll(first, 40 * q, 1)[:, :384] for q in range(window // 8)], axis=0
    ).astype(jnp.bfloat16)[:, :rows]
    row = lax.broadcasted_iota(jnp.int32, (2 * bins, window), 0)
    col = lax.broadcasted_iota(jnp.int32, (2 * bins, window), 1)
    place = row % mine
    order = row // mine
    holder = (order % chips) * 2 + order // chips
    freq = holder * (mine // 2) + place % (mine // 2) + 1
    time = me * steps - lead + col
    turn = (freq * time + jnp.where(place >= mine // 2, length // 4, 0)) & (length - 1)
    table = jnp.cos(turn.astype(jnp.float32) * (2.0 * math.pi / length))
    table = jnp.where((time >= 0) & (time < length), table, 0.0)
    table_high, table_low = split(table)
    gmap = mm(table_high, banded) + mm(table_low, banded)
    gmap_high, gmap_low = split(gmap)

    for load in loaded:
        load.wait()
    chunk = 256

    def transform(c):
        halves = []
        for h in range(2):
            part = raw_ref[:, h * hc + c * chunk : h * hc + (c + 1) * chunk]
            spectra = mm(gmap_high, part) + mm(gmap_low, part)
            halves.append(spectra.reshape(n, mine, chunk))
        both[:, :, c * chunk : (c + 1) * chunk] = jnp.concatenate(halves, axis=1).astype(
            jnp.bfloat16
        )

    pieces = [(0, hc // 2), (hc // 2, hc // 2 + 128)]
    for c in range(hc // chunk // 2):
        transform(c)
    line = lax.broadcasted_iota(jnp.int32, (2 * mine, 128), 0)
    info = jnp.zeros((2 * mine, 128), jnp.float32)
    for d in range(bands):
        listed = jnp.int32(0)
        for s in range(bands):
            hit = (plan_ref[s] == d + 1) & (s < plan_ref[2 * bands])
            listed = listed + hit.astype(jnp.int32)
        info = jnp.where(line == core * mine + d, listed.astype(jnp.float32), info)
    both[:, :, hc:] = jnp.broadcast_to(info[None], (n, 2 * mine, 128)).astype(jnp.bfloat16)

    pl.semaphore_wait(barrier, n - 1)

    def copy0(p):
        cols = pl.ds(*pieces[p])
        return pltpu.make_async_remote_copy(
            src_ref=both.at[pl.ds((1 - core) * chips, chips), :, cols],
            dst_ref=pair.at[:, :, cols], send_sem=ss0.at[p], recv_sem=rs0.at[p],
            device_id={"chan": chip * 2 + 1 - core}, device_id_type=MESH,
        )

    def copy1(p, k):
        to = lax.rem(chip + k, chips)
        cols = pl.ds(*pieces[p])
        return pltpu.make_async_remote_copy(
            src_ref=send1.at[to, :, cols], dst_ref=recv1.at[chip, :, cols],
            send_sem=ss1.at[p * chips + k], recv_sem=rs1.at[p * chips + k],
            device_id={"chan": to * 2 + core}, device_id_type=MESH,
        )

    second_copy = pltpu.make_async_remote_copy(
        src_ref=both2.at[pl.ds((1 - core) * chips, chips)], dst_ref=pair2, send_sem=ss4,
        recv_sem=rs4, device_id={"chan": chip * 2 + 1 - core}, device_id_type=MESH,
    )

    def copy2(k):
        to = lax.rem(chip + k, chips)
        return pltpu.make_async_remote_copy(
            src_ref=send2.at[to], dst_ref=recv2.at[chip], send_sem=ss2.at[k],
            recv_sem=rs2.at[k], device_id={"chan": to * 2 + core}, device_id_type=MESH,
        )

    share = block // n
    place = (core * chips + chip) * share

    def copy3(k):
        to = lax.rem(me + k, n)
        return pltpu.make_async_remote_copy(
            src_ref=send3.at[to], dst_ref=out_ref.at[0, pl.ds(place, share)],
            send_sem=ss3.at[k], recv_sem=rs3.at[k], device_id={"chan": to}, device_id_type=MESH,
        )

    copy0(0).start()
    for c in range(hc // chunk // 2, hc // chunk):
        transform(c)
    copy0(1).start()
    for p in range(2):
        cols = slice(pieces[p][0], sum(pieces[p]))
        copy0(p).wait_recv()
        for k in range(1, chips):
            to = lax.rem(chip + k, chips)
            own = both[core * chips + to, :, cols].astype(jnp.float32)
            send1[to, :, cols] = (own + pair[to, :, cols].astype(jnp.float32)).astype(jnp.bfloat16)
            copy1(p, k).start()
        own = both[core * chips + chip, :, cols].astype(jnp.float32)
        recv1[chip, :, cols] = (own + pair[chip, :, cols].astype(jnp.float32)).astype(jnp.bfloat16)
    for p in range(2):
        for k in range(1, chips):
            copy1(p, k).wait_recv()
    total = recv1[0, :, :hc].astype(jnp.float32)
    for i in range(1, chips):
        total = total + recv1[i, :, :hc].astype(jnp.float32)

    white = []
    for j in range(n):
        h, at = divmod(j * block, hc)
        part = total[h * mine : (h + 1) * mine, at : at + block]
        squares = part * part
        squares = squares + pltpu.roll(squares, mine // 2, 0)
        power = jnp.sum(squares, axis=1, keepdims=True) / (2 * block)
        white.append(part * lax.rsqrt(power + 1e-06))
    left = jnp.concatenate(white, axis=0).astype(jnp.bfloat16)
    weights = [recv1[i, :, hc:].astype(jnp.float32) for i in range(chips)]
    rights = []
    for d in range(bands):
        tiles = []
        for i in range(n):
            if i + d + 1 < n:
                tiles.append(white[i + d + 1] * weights[i // 2][i % 2 * mine + d : i % 2 * mine + d + 1, :])
            else:
                tiles.append(jnp.zeros((mine, block), jnp.float32))
        rights.append(jnp.concatenate(tiles, axis=0).astype(jnp.bfloat16))
    right = jnp.concatenate(rights, axis=1)
    stacks = lax.dot_general(
        left, right, (((0,), (0,)), ((), ())), preferred_element_type=jnp.float32
    )
    hb = bands // 2 * block
    stacks = jnp.concatenate(
        [stacks[:, :hb].reshape(n, share, hb), stacks[:, hb:].reshape(n, share, hb)], axis=1
    )
    both2[...] = stacks.astype(jnp.bfloat16)

    second_copy.start()
    second_copy.wait_recv()
    for k in range(1, chips):
        to = lax.rem(chip + k, chips)
        own = both2[core * chips + to].astype(jnp.float32)
        send2[to] = (own + pair2[to].astype(jnp.float32)).astype(jnp.bfloat16)
        copy2(k).start()
    own = both2[core * chips + chip].astype(jnp.float32)
    recv2[chip] = (own + pair2[chip].astype(jnp.float32)).astype(jnp.bfloat16)
    for k in range(1, chips):
        copy2(k).wait_recv()
    total = recv2[0].astype(jnp.float32)
    for i in range(1, chips):
        total = total + recv2[i].astype(jnp.float32)
    total = total * (1.0 / (2 * bins))

    for to in range(n):
        chosen = jnp.zeros((share, block), jnp.float32)
        for d in range(bands):
            h, at = divmod(d * block, hb)
            owned = (plan_ref[bands + d] == to).astype(jnp.float32)
            chosen = chosen + total[h * share : (h + 1) * share, at : at + block] * owned
        send3[to] = chosen
    for k in range(1, n):
        copy3(k).start()
    out_ref[0, pl.ds(place, share)] = send3[me]
    for k in range(1, n):
        copy3(k).wait_recv()
    for p in range(2):
        copy0(p).wait_send()
        for k in range(1, chips):
            copy1(p, k).wait_send()
    second_copy.wait_send()
    for k in range(1, chips):
        copy2(k).wait_send()
    for k in range(1, n):
        copy3(k).wait_send()


def fused(raw, taps, tile_dist, tile_count, owner):
    n = lax.axis_size("chan")
    rows, channels = raw.shape
    width = taps.shape[0]
    half = (width - 1) // 2
    bands = tile_dist.shape[1]
    block = channels // n
    steps = rows // 5
    mine = 2 * (steps * n // 16) // n
    lead = (128 - steps) // 2
    lanes = 1024
    start = lanes - 5 * lead - half
    line = jnp.pad(taps.astype(jnp.float32), (start, lanes - start - width))
    line = line[None]
    plan = jnp.concatenate([tile_dist[0], owner, tile_count])
    vmem, hbm = pl.BlockSpec(memory_space=pltpu.VMEM), pl.BlockSpec(memory_space=pltpu.HBM)
    share = block // n
    sems = [pltpu.SemaphoreType.DMA((n,)) for _ in range(6)]
    return pl.pallas_call(
        functools.partial(fused_kernel, n, width, bands),
        out_shape=jax.ShapeDtypeStruct((1, block, block), jnp.float32),
        in_specs=[hbm, hbm, vmem],
        out_specs=vmem,
        scratch_shapes=[
            pltpu.SMEM(plan.shape, jnp.int32),
            pltpu.VMEM(raw.shape, raw.dtype),
            pltpu.SemaphoreType.DMA((2,)),
            pltpu.VMEM((n, 2 * mine, channels // 2 + 128), jnp.bfloat16),
            pltpu.VMEM((n // 2, 2 * mine, channels // 2 + 128), jnp.bfloat16),
            pltpu.VMEM((n // 2, 2 * mine, channels // 2 + 128), jnp.bfloat16),
            pltpu.VMEM((n // 2, 2 * mine, channels // 2 + 128), jnp.bfloat16),
            pltpu.VMEM((n, 2 * share, bands // 2 * block), jnp.bfloat16),
            pltpu.VMEM((n // 2, 2 * share, bands // 2 * block), jnp.bfloat16),
            pltpu.VMEM((n // 2, 2 * share, bands // 2 * block), jnp.bfloat16),
            pltpu.VMEM((n // 2, 2 * share, bands // 2 * block), jnp.bfloat16),
            pltpu.VMEM((n, share, block), jnp.float32),
            pltpu.SemaphoreType.DMA((2,)),
            pltpu.SemaphoreType.DMA((2,)),
            pltpu.SemaphoreType.DMA,
            pltpu.SemaphoreType.DMA,
            *sems,
        ],
        compiler_params=pltpu.CompilerParams(
            collective_id=0, has_side_effects=True, vmem_limit_bytes=int(53.25 * 2**20)
        ),
    )(plan, raw, line)


def shards(raw, taps, tile_dist, tile_count, owner):
    n = lax.axis_size("chan")
    rows, channels = raw.shape
    steps = rows // 5
    fits = (
        channels == 128 * n
        and n == 16
        and rows == 320
        and taps.shape[0] == 255
        and tile_dist.shape[1] == 4
    )
    path = fused if fits else streamed
    return path(raw, taps, tile_dist, tile_count, owner)


def solution(mesh):
    in_specs = (P("chan", "groups"), P(), P("chan", "groups"), P(("groups", "chan")), P("groups"))
    out_specs = P("chan", "groups", None)
    return jax.shard_map(shards, mesh=mesh, in_specs=in_specs, out_specs=out_specs, check_vma=False)
```
